32 devices in a mesh: groups: 2 (over y), tm: 16 (over z, x, core).
Axes of the slice: x: 2, y: 2, z: 4, core: 2. Of those that a mesh axis runs over, the one named last changes fastest.
Arguments:
- observations: float32 [512, 16, 256], P(('groups', 'tm')), parts along dimension 0, may hold values from -6 to 6
- start_mean: float32 [32, 512], P('groups'), parts along dimension 0, may hold values from -6 to 6
- transition: float32 [512, 512], replicated, may hold values from -0.01 to 1
- obs_map: float32 [512, 256], replicated, may hold values from -0.009765625 to 0.009765625
- kalman_gain: float32 [256, 512], replicated, may hold values from -0.01171875 to 0.01171875
- smoother_gain: float32 [512, 512], replicated, may hold values from -0.01 to 1
Outputs:
- filtered: float32 [512, 16, 512], P(('groups', 'tm')), parts along dimension 0
- smoothed: float32 [512, 16, 512], P(('groups', 'tm')), parts along dimension 0
The draws below stay inside these ranges and needn't reach their ends.
There are 2 independent parts, one for each index of `groups`. The reference program is written for one: setup_inputs(seed, part) draws one part's arguments, and reference() takes and returns one part's arrays. A program takes and returns all parts, laid end to end along the dimension named above; an argument that names none is the same for every part. Nothing has to cross between parts.
All inputs are finite; a program needn't handle non-finite values.
Results may differ from the reference program's by a relative error of at most 0.0003.
Values sent between devices are 32-bit elements; how exact they have to be, the bound alone decides.
A program may use at most 64 MiB of HBM per device.

```python
import math
import jax
import jax.numpy as jnp
from jax import lax

NS = 512
NY = 256
TS = 16
B = 16
T_SIZE = 256
N_TM = 16


def diagonal_heavy(key, slow_share):
    first_key, second_key, third_key, fourth_key = jax.random.split(key, 4)
    chain_steps = TS * N_TM
    slow_total = jnp.exp(jax.random.uniform(first_key, (NS,), jnp.float32, math.log(0.1), math.log(2.0)))
    fast_length = jnp.exp(jax.random.uniform(second_key, (NS,), jnp.float32, math.log(30.0), math.log(50.0)))
    slow_pick = jax.random.bernoulli(third_key, slow_share, (NS,))
    rates = jnp.where(slow_pick, slow_total / chain_steps, 1.0 / fast_length)
    decay_rates = jnp.exp(-rates)
    spread_part = jax.random.truncated_normal(fourth_key, -4.0, 4.0, (NS, NS), jnp.float32)
    spread_scale = 0.15 / (chain_steps * math.sqrt(NS))
    return spread_part * spread_scale + jnp.diag(decay_rates)


def draw_transition(key, part):
    share = 0.5
    return diagonal_heavy(jax.random.fold_in(key, 17), share)


def draw_smoother_gain(key, part):
    share = 0.5
    return diagonal_heavy(jax.random.fold_in(key, 29), share)


def steps_of(rng, extent, pieces, smallest, high):
    def one(position, shards_of):
        steps = jax.random.uniform(jax.random.fold_in(jax.random.fold_in(rng, 6), position), (shards_of,), jnp.float32, smallest / len(pieces), high / len(pieces))
        return jnp.repeat(jnp.exp(steps), extent[position] // shards_of).reshape((-1,) + (1,) * (len(extent) - position - 1))

    level = one(*pieces[0])
    for cut in pieces[1:]:
        level = level * one(*cut)
    return level


def bell_draw(own_key, shape, width, reach, pieces=(), kind=jnp.bfloat16):
    array = width * jax.random.normal(own_key, shape, jnp.float32)
    if pieces:
        array = array * steps_of(own_key, shape, pieces, -0.22, 0.18)
    return jnp.clip(array, -reach, reach).astype(kind)


def setup_inputs(seed: int = 0, part: int = 0) -> dict:
    seeds = jax.random.split(jax.random.key(seed), 7)
    part_keys = jax.random.split(jax.random.fold_in(seeds[6], part), 7)
    return {
        "observations": bell_draw(part_keys[0], (T_SIZE, B, NY), 1.0, 6.0, ((0, 16),), jnp.float32),
        "start_mean": bell_draw(part_keys[1], (B, NS), 1.0, 6.0, (), jnp.float32),
        "transition": draw_transition(jax.random.fold_in(seeds[6], 71), part),
        "obs_map": bell_draw(seeds[3], (NS, NY), (3 * NS * TS * N_TM) ** -0.5, 0.009765625, (), jnp.float32),
        "kalman_gain": bell_draw(seeds[4], (NY, NS), (4 * NY * TS * N_TM) ** -0.5, 0.01171875, (), jnp.float32),
        "smoother_gain": draw_smoother_gain(jax.random.fold_in(seeds[6], 71), part),
    }


def product(first_op, second_op):
    return jnp.dot(first_op, second_op, precision=lax.Precision.HIGHEST, preferred_element_type=jnp.float32)


def reference(observations, start_mean, transition, obs_map, kalman_gain, smoother_gain):
    def advance(carried, observed):
        predicted = product(carried, transition)
        updated = predicted + product(observed - product(predicted, obs_map), kalman_gain)
        return updated, updated

    last_state, filtered = lax.scan(advance, start_mean.astype(jnp.float32), observations)

    def retreat(carried, current):
        smoothed_now = current + product(carried - product(current, transition), smoother_gain)
        return smoothed_now, smoothed_now

    top_carry = product(last_state, transition)
    unused, smoothed = lax.scan(retreat, top_carry, filtered, reverse=True)
    return filtered, smoothed
```

```python
import functools

import jax
import jax.numpy as jnp
from jax import lax
from jax.experimental import pallas as pl
from jax.experimental.pallas import tpu as pltpu
from jax.sharding import PartitionSpec as P

MESH = pl.DeviceIdType.MESH


def log2(n):
    return n.bit_length() - 1


def radices_of(bits):
    return [2] * (bits // 2) + [1] * (bits % 2)


def messages_of(devices):
    rounds = radices_of(log2(devices))
    out, stride = [], 1
    for r, bits in enumerate(rounds):
        last = r == len(rounds) - 1
        for term in range(2**bits):
            distance = term * stride + (1 if last else 0)
            if 0 < distance < devices:
                out.append((r, term, distance))
        stride *= 2**bits
    return out


def mm(a, b):
    return jnp.dot(a, b, preferred_element_type=jnp.float32)


def split(x):
    high = x.astype(jnp.bfloat16)
    return high, (x - high.astype(jnp.float32)).astype(jnp.bfloat16)


def product(a, w):
    high, low = split(a)
    rows = a.shape[0]
    both = mm(jnp.concatenate([high, low], axis=0), w[0])
    return both[:rows] + both[rows:] + mm(high, w[1])


def apply(a, w):
    return a + product(a, w)


def less_identity(m):
    row = lax.broadcasted_iota(jnp.int32, m.shape, 0)
    column = lax.broadcasted_iota(jnp.int32, m.shape, 1)
    return m - jnp.where(row == column, 1.0, 0.0)


def keep(w, x):
    w[0], w[1] = split(x)


def square(dst, src, tile=256):
    def body(i, c):
        rows = pl.ds(pl.multiple_of(i * tile, tile), tile)
        high, low = src[0, rows, :], src[1, rows, :]
        x = mm(high, src[0]) + mm(low, src[0]) + mm(high, src[1])
        e = high.astype(jnp.float32) + low.astype(jnp.float32)
        dst[0, rows, :], dst[1, rows, :] = split(x + 2.0 * e)
        return c

    lax.fori_loop(0, src.shape[1] // tile, body, 0)


def kernel(devices, steps, y_ref, start_ref, a_ref, h_ref, k_ref, g_ref, f_out, s_out,
           aw, hw, kw, fpow, gpow, x, z, ends, inbox, send_sem, recv_sem):
    me = lax.axis_index("tm")
    b = start_ref.shape[0]
    local_bits, hop_bits = log2(steps), log2(devices)
    rounds = radices_of(hop_bits)
    messages = messages_of(devices)
    distances = sorted({m[2] for m in messages})

    barrier = pltpu.get_barrier_semaphore()
    for d in distances:
        for sign in (1, -1):
            other = me + sign * d

            @pl.when((other >= 0) & (other < devices))
            def _():
                pl.semaphore_signal(barrier, inc=1, device_id={"tm": other}, device_id_type=MESH)

    keep(aw, less_identity(a_ref[...]))
    keep(hw, h_ref[...])
    keep(kw, k_ref[...])
    keep(gpow.at[0], less_identity(g_ref[...]))
    x[...] = product(y_ref[...], kw)
    h = h_ref[...] + product(less_identity(a_ref[...]), hw)
    keep(fpow.at[0], less_identity(a_ref[...]) - product(h, kw))

    @pl.when(me == 0)
    def _():
        x[:b, :] += apply(start_ref[...], fpow.at[0])

    for j in range(local_bits):
        shift = b << j
        x[shift:, :] += apply(x[:-shift, :], fpow.at[j])
        square(fpow.at[j + 1], fpow.at[j])

    peers = 0
    for d in distances:
        peers += jnp.where(me >= d, 1, 0) + jnp.where(me + d < devices, 1, 0)
    pl.semaphore_wait(barrier, peers)

    def copy(way, r, index, distance):
        return pltpu.make_async_remote_copy(
            src_ref=ends.at[way, r],
            dst_ref=inbox.at[way, index],
            send_sem=send_sem.at[way, index],
            recv_sem=recv_sem.at[way, index],
            device_id={"tm": me + distance * (1 - 2 * way)},
            device_id_type=MESH,
        )

    def exchange(way, value, powers, beside):
        sends = lambda d: (me + d < devices) if way == 0 else (me >= d)
        gets = lambda d: (me >= d) if way == 0 else (me + d < devices)
        level = 0
        for r, bits in enumerate(rounds):
            ends[way, r] = value
            mine = [(i, m[1], m[2]) for i, m in enumerate(messages) if m[0] == r]
            for i, term, d in mine:
                @pl.when(sends(d))
                def _():
                    copy(way, r, i, d).start()

                @pl.when(jnp.logical_not(gets(d)))
                def _():
                    inbox[way, i] = jnp.zeros(inbox.shape[2:], jnp.float32)
            beside(r)
            for i, term, d in mine:
                @pl.when(gets(d))
                def _():
                    copy(way, r, i, d).wait_recv()
            terms = {0: value}
            for i, term, d in mine:
                terms[term] = inbox[way, i]
            terms = [terms.get(t, jnp.zeros_like(value)) for t in range(2**bits)]
            for k in range(bits):
                odd = jnp.concatenate(terms[1::2], axis=0) if len(terms) > 2 else terms[1]
                moved = apply(odd, powers.at[level + k])
                terms = [terms[2 * i] + moved[i * b:(i + 1) * b] for i in range(len(terms) // 2)]
            value = terms[0]
            level += bits
        for i, m in enumerate(messages):
            @pl.when(sends(m[2]))
            def _():
                copy(way, m[0], i, m[2]).wait_send()
        return value

    def beside_forward(r):
        done = sum(rounds[:r])
        first = [local_bits + done + k for k in range(rounds[r] - (1 if r == 0 else 0))]
        for j in first:
            if j + 1 < local_bits + hop_bits and r == 0:
                square(fpow.at[j + 1], fpow.at[j])
        if r == 0:
            for j in range(local_bits):
                square(gpow.at[j + 1], gpow.at[j])
        if r > 0:
            for j in range(local_bits + done - 1, local_bits + done + rounds[r] - 1):
                square(fpow.at[j + 1], fpow.at[j])

    entering = exchange(0, x[-b:, :], fpow.at[pl.ds(local_bits, hop_bits)], beside_forward)

    z[:b, :] = apply(entering, fpow.at[0])
    for j in range(local_bits):
        n = b << j
        z[n:2 * n, :] = apply(z[:n, :], fpow.at[j])
    x[...] += z[...]
    f_out[...] = x[...]
    last = x[-b:, :]
    step = product(x[...], aw)
    x[...] = -step - product(x[...] + step, gpow.at[0])

    @pl.when(me == devices - 1)
    def _():
        x[-b:, :] = last

    for j in range(local_bits):
        shift = b << j
        x[:-shift, :] += apply(x[shift:, :], gpow.at[j])

    def beside_backward(r):
        done = sum(rounds[:r])
        for j in range(local_bits + max(done - 1, 0), local_bits + done + rounds[r] - 1):
            square(gpow.at[j + 1], gpow.at[j])

    leaving = exchange(1, x[:b, :], gpow.at[pl.ds(local_bits, hop_bits)], beside_backward)
    total = b * steps
    z[total - b:, :] = apply(leaving, gpow.at[0])
    for j in range(local_bits):
        n = b << j
        z[total - 2 * n:total - n, :] = apply(z[total - n:, :], gpow.at[j])
    s_out[...] = x[...] + z[...]


def per_device(devices, y, start, a, h, k, g):
    steps, b, ny = y.shape
    ns = a.shape[0]
    powers = log2(steps) + log2(devices)
    count = len(messages_of(devices))
    two = lambda *shape: pltpu.VMEM((2,) + shape, jnp.bfloat16)
    rows = steps * b
    f, s = pl.pallas_call(
        functools.partial(kernel, devices, steps),
        out_shape=[jax.ShapeDtypeStruct((rows, ns), jnp.float32)] * 2,
        in_specs=[pl.BlockSpec(memory_space=pltpu.VMEM)] * 6,
        out_specs=[pl.BlockSpec(memory_space=pltpu.VMEM)] * 2,
        scratch_shapes=[
            two(ns, ns), two(ns, ny), two(ny, ns),
            pltpu.VMEM((powers, 2, ns, ns), jnp.bfloat16),
            pltpu.VMEM((powers, 2, ns, ns), jnp.bfloat16),
            pltpu.VMEM((rows, ns), jnp.float32),
            pltpu.VMEM((rows, ns), jnp.float32),
            pltpu.VMEM((2, len(radices_of(log2(devices))), b, ns), jnp.float32),
            pltpu.VMEM((2, count, b, ns), jnp.float32),
            pltpu.SemaphoreType.DMA((2, count)),
            pltpu.SemaphoreType.DMA((2, count)),
        ],
        compiler_params=pltpu.CompilerParams(
            collective_id=0, has_side_effects=True, vmem_limit_bytes=56 * 1024 * 1024
        ),
    )(y.reshape(rows, ny), start, a, h, k, g)
    return f.reshape(steps, b, ns), s.reshape(steps, b, ns)


def solution(mesh):
    in_specs = (P(("groups", "tm"), None, None), P("groups", None), P(), P(), P(), P())
    out_specs = (P(("groups", "tm"), None, None), P(("groups", "tm"), None, None))
    return jax.shard_map(
        functools.partial(per_device, mesh.shape["tm"]),
        mesh=mesh, in_specs=in_specs, out_specs=out_specs, check_vma=False,
    )
```
